512 devices in a mesh: head: 8 (over y_lo, core), ctx: 64 (over z, x, y_hi).
Axes of the slice: x: 4, y: 8 (y_hi: 2, y_lo: 4; y = y_hi * 4 + y_lo), z: 8, core: 2. Of those that a mesh axis runs over, the one named last changes fastest.
Arguments:
- queries: bfloat16 [12288, 2048], P(('head', 'ctx')), may hold values from -40 to 40
- keys: bfloat16 [12288, 2048], P(('head', 'ctx')), may hold values from -8 to 8
- values: bfloat16 [12288, 2048], P(('head', 'ctx')), may hold values from -6 to 6
Outputs:
- attended: bfloat16 [12288, 2048], P(('head', 'ctx'))
The draws below stay inside these ranges and needn't reach their ends.
All inputs are finite; a program needn't handle non-finite values.
Results may differ from the reference program's by a relative error of at most 0.0095.
Values may be sent and summed in bfloat16 or wider, within the bound.
No kernel may reach another device: no remote copies, remote signals or barrier semaphores. Data moves between devices by JAX's collectives and lax.ppermute only.
A program may use at most 64 MiB of HBM per device.

```python
import math
import jax
import jax.numpy as jnp
from jax import lax

HEADS = 16
HD = 128
LEN = 12288


def draw_queries(key, part):
    key = jax.random.fold_in(key, 11)
    result = 2.5 * jnp.clip(jax.random.normal(key, (LEN, HEADS * HD), jnp.float32), -4.0, 4.0)
    return result.astype(jnp.bfloat16)


def draw_keys(key, part):
    key = jax.random.fold_in(key, 23)
    result = jnp.clip(jax.random.normal(key, (LEN, HEADS * HD), jnp.float32), -4.0, 4.0)
    return result.astype(jnp.bfloat16)


def levels(stream_key, shape, pieces, least, top_value):
    level, own = 1.0, jax.random.fold_in(stream_key, 6)
    for dim, parts in pieces:
        steps = jnp.exp(jax.random.uniform(jax.random.fold_in(own, dim), (parts,), jnp.float32, least / len(pieces), top_value / len(pieces)))
        level = level * jnp.repeat(steps, shape[dim] // parts).reshape([-1 if axis == dim else 1 for axis in range(len(shape))])
    return level


def scatter_about(own_key, extent, spread, limit, cuts=(), dtype=jnp.bfloat16):
    values = jax.random.normal(own_key, extent, jnp.float32) * spread
    if len(cuts) > 0:
        values = levels(own_key, extent, cuts, -0.22, 0.18) * values
    return jnp.clip(values, min=-limit, max=limit).astype(dtype)


def setup_inputs(seed: int = 0) -> dict:
    key_of = jax.random.split(jax.random.key(seed), 4)
    return {
        "queries": draw_queries(jax.random.fold_in(key_of[3], 71), 0),
        "keys": draw_keys(jax.random.fold_in(key_of[3], 71), 0),
        "values": scatter_about(key_of[2], (LEN, HEADS * HD), 1.0, 6.0, ((0, 512),)),
    }


def reference(queries, keys, values):
    block_rows = math.gcd(LEN, 512)

    def by_head(array):
        return array.reshape(LEN, HEADS, HD).transpose(1, 0, 2)

    def one_head(triple):
        query_head, key_head, value_head = triple
        blocks = query_head.reshape(LEN // block_rows, block_rows, HD)

        def one_block(query_block):
            scores = jnp.dot(query_block, key_head.T, preferred_element_type=jnp.float32) * (1.0 / math.sqrt(HD))
            weights = jnp.exp(scores - lax.optimization_barrier(jnp.max(scores, axis=1, keepdims=True)))
            totals = lax.optimization_barrier(jnp.sum(weights, axis=1, keepdims=True))
            numerator = jnp.dot(weights.astype(jnp.bfloat16), value_head, preferred_element_type=jnp.float32)
            return numerator / totals
        return lax.map(one_block, blocks).reshape(LEN, HD)
    result = lax.map(one_head, (by_head(queries), by_head(keys), by_head(values)))
    result = result.transpose(1, 0, 2)
    return result.reshape(LEN, HEADS * HD).astype(jnp.bfloat16)
```

```python
import functools
import math

import jax
import jax.numpy as jnp
from jax import lax
from jax.experimental import pallas as pl
from jax.experimental.pallas import tpu as pltpu
from jax.sharding import Mesh, PartitionSpec as P

HD = 128
HEADS = 16
TOKENS = 24
SIDE = 8
SCALE = math.log2(math.e) / math.sqrt(HD)
VMEM = pltpu.CompilerParams(vmem_limit_bytes=48 * 1024 * 1024)

AXES = ("yl", "c", "zh", "zl", "x", "yh")
SIZES = (4, 2, 4, 2, 4, 2)
HEAD_GROUP = ("yh", "yl", "zl")
BACK_GROUP = ("zh", "yh", "yl", "zl")


def whole(count):
    return [pl.BlockSpec(memory_space=pltpu.VMEM)] * count


def pack_kernel(q_ref, k_ref, v_ref, out_ref):
    for head in range(HEADS):
        columns = slice(head * HD, (head + 1) * HD)
        out_ref[head, :, 0:HD] = q_ref[:, columns]
        out_ref[head, :, HD : 2 * HD] = k_ref[:, columns]
        out_ref[head, :, 2 * HD : 3 * HD] = v_ref[:, columns]


def pack(queries, keys, values):
    return pl.pallas_call(
        pack_kernel,
        out_shape=jax.ShapeDtypeStruct((HEADS, TOKENS, 3 * HD), jnp.bfloat16),
        in_specs=whole(3),
        out_specs=pl.BlockSpec(memory_space=pltpu.VMEM),
        compiler_params=VMEM,
        name="pack",
    )(queries, keys, values)


def attend_kernel(q_ref, kv0_ref, kv1_ref, out_ref, keys_ref, wide_ref, scores_ref, *, rows):
    half = kv0_ref.shape[0]
    for part, kv_ref in enumerate((kv0_ref, kv1_ref)):
        span = slice(part * half, (part + 1) * half)
        keys_ref[span, :] = kv_ref[:, :HD]
        wide_ref[span, :HD] = kv_ref[:, HD:]
    wide_ref[:, HD:] = jnp.ones((2 * half, HD), jnp.bfloat16)
    count = q_ref.shape[0] // rows
    blocks = rows // TOKENS
    lane = lax.broadcasted_iota(jnp.int32, (blocks, SIDE, HD), 2)

    def scores(step):
        return lax.dot_general(
            q_ref[step * rows : (step + 1) * rows, :],
            keys_ref[...],
            (((1,), (1,)), ((), ())),
            preferred_element_type=jnp.float32,
        )

    def finish(step, tile):
        top = jnp.max(tile, axis=1, keepdims=True)
        weights = jnp.exp2((tile - top) * SCALE).astype(jnp.bfloat16)
        sums = jnp.dot(weights, wide_ref[...], preferred_element_type=jnp.float32)
        total = sums[:, HD:]
        share = (sums[:, :HD] / total).reshape(blocks, TOKENS, HD)
        rest = (jnp.log2(total) + top * SCALE).reshape(blocks, TOKENS, HD)
        side = jnp.zeros((blocks, SIDE, HD), jnp.float32)
        for term in range(3):
            piece = rest.astype(jnp.bfloat16).astype(jnp.float32)
            rest = rest - piece
            for group in range(TOKENS // SIDE):
                side = jnp.where(
                    lane == group * 3 + term, piece[:, group * SIDE : (group + 1) * SIDE, :], side
                )
        out_ref[step * blocks : (step + 1) * blocks] = jnp.concatenate([share, side], axis=1).astype(
            jnp.bfloat16
        )

    scores_ref[0] = scores(0)
    for step in range(count):
        if step + 1 < count:
            scores_ref[(step + 1) % 2] = scores(step + 1)
        finish(step, scores_ref[step % 2])


def attend(query, kv0, kv1, rows=192):
    count = query.shape[0]
    half = kv0.shape[0]
    return pl.pallas_call(
        functools.partial(attend_kernel, rows=rows),
        out_shape=jax.ShapeDtypeStruct((count // TOKENS, TOKENS + SIDE, HD), jnp.bfloat16),
        in_specs=whole(3),
        out_specs=pl.BlockSpec(memory_space=pltpu.VMEM),
        scratch_shapes=[
            pltpu.VMEM((2 * half, HD), jnp.bfloat16),
            pltpu.VMEM((2 * half, 2 * HD), jnp.bfloat16),
            pltpu.VMEM((2, rows, 2 * half), jnp.float32),
        ],
        compiler_params=VMEM,
        cost_estimate=pl.CostEstimate(
            flops=8 * count * half * HD, bytes_accessed=4 << 20, transcendentals=2 * count * half
        ),
        name="attend",
    )(query, kv0, kv1)


def combine_kernel(parts_ref, out_ref):
    for head in range(HEADS):
        blocks = [parts_ref[part * HEADS + head].astype(jnp.float32) for part in range(4)]
        for group in range(TOKENS // SIDE):
            rows = slice(group * SIDE, (group + 1) * SIDE)
            logs = []
            for block in blocks:
                side = block[TOKENS:, group * 3 : group * 3 + 3]
                logs.append(side[:, 0:1] + side[:, 1:2] + side[:, 2:3])
            top = jnp.maximum(jnp.maximum(logs[0], logs[1]), jnp.maximum(logs[2], logs[3]))
            factors = [jnp.exp2(log - top) for log in logs]
            total = factors[0] + factors[1] + factors[2] + factors[3]
            acc = blocks[0][rows] * (factors[0] / total)
            for part in range(1, 4):
                acc = acc + blocks[part][rows] * (factors[part] / total)
            out_ref[rows, head * HD : (head + 1) * HD] = acc


def combine(parts):
    return pl.pallas_call(
        combine_kernel,
        out_shape=jax.ShapeDtypeStruct((TOKENS, HEADS * HD), jnp.float32),
        in_specs=whole(1),
        out_specs=pl.BlockSpec(memory_space=pltpu.VMEM),
        compiler_params=VMEM,
        name="combine",
    )(parts)


def shift(axis, by, size):
    return [(source, (source + by) % size) for source in range(size)]


def per_device(queries, keys, values):
    packed = pack(queries, keys, values)
    mine = lax.all_to_all(packed, HEAD_GROUP, split_axis=0, concat_axis=0, tiled=True)
    mine = mine.reshape(HEADS * TOKENS, 3 * HD)
    own_q = mine[:, :HD]
    own_kv = mine[:, HD:]
    others = [lax.ppermute(own_q, "zh", shift("zh", by, 4)) for by in (1, 2, 3)]
    kv = lax.all_to_all(
        jnp.broadcast_to(own_kv[None], (4,) + own_kv.shape), "x", split_axis=0, concat_axis=0, tiled=True
    ).reshape(4 * own_kv.shape[0], 2 * HD)
    other_kv = lax.ppermute(kv, "c", [(0, 1), (1, 0)])
    query = jnp.concatenate([own_q] + others, axis=0)
    parts = attend(query, kv, other_kv)
    me = lax.axis_index("zh")
    slots = parts.reshape(4, HEADS, TOKENS + SIDE, HD)
    slots = jnp.take(slots, (me - jnp.arange(4)) % 4, axis=0)
    sent = lax.all_to_all(
        slots.reshape(parts.shape), BACK_GROUP, split_axis=0, concat_axis=0, tiled=True
    )
    return combine(sent).astype(jnp.bfloat16)


def solution(mesh):
    fine = Mesh(mesh.devices.reshape(SIZES), AXES)
    placed = P(AXES, None)
    return jax.shard_map(
        per_device, mesh=fine, in_specs=(placed,) * 3, out_specs=placed, check_vma=False
    )
```

```python
import functools
import math

import jax
import jax.numpy as jnp
from jax import lax
from jax.experimental import pallas as pl
from jax.experimental.pallas import tpu as pltpu
from jax.sharding import Mesh, PartitionSpec as P

HD = 128
HEADS = 16
TOKENS = 24
SIDE = 8
SCALE = math.log2(math.e) / math.sqrt(HD)
VMEM = pltpu.CompilerParams(vmem_limit_bytes=48 * 1024 * 1024)

AXES = ("yl", "c", "zh", "zl", "x", "yh")
SIZES = (4, 2, 4, 2, 4, 2)
HEAD_GROUP = ("yh", "yl", "zl")
BACK_GROUP = ("zh", "yh", "yl", "zl")


def whole(count):
    return [pl.BlockSpec(memory_space=pltpu.VMEM)] * count


def pack_kernel(q_ref, k_ref, v_ref, out_ref, near_ref, done):
    copies = [
        pltpu.make_async_copy(source, near_ref.at[place], done.at[place])
        for place, source in enumerate((q_ref, k_ref, v_ref))
    ]
    for copy in copies:
        copy.start()
    for place, copy in enumerate(copies):
        copy.wait()
        for head in range(HEADS):
            out_ref[head, :, place * HD : (place + 1) * HD] = near_ref[
                place, :, head * HD : (head + 1) * HD
            ]


def pack(queries, keys, values):
    return pl.pallas_call(
        pack_kernel,
        out_shape=jax.ShapeDtypeStruct((HEADS, TOKENS, 3 * HD), jnp.bfloat16),
        in_specs=[pl.BlockSpec(memory_space=pl.ANY)] * 3,
        out_specs=pl.BlockSpec(memory_space=pltpu.VMEM),
        scratch_shapes=[
            pltpu.VMEM((3, TOKENS, HEADS * HD), jnp.bfloat16),
            pltpu.SemaphoreType.DMA((3,)),
        ],
        name="pack",
    )(queries, keys, values)


def load_keys(kv_ref, keys_ref, wide_ref):
    keys_ref[...] = kv_ref[:, :HD]
    wide_ref[:, :HD] = kv_ref[:, HD:]
    wide_ref[:, HD:] = jnp.ones((kv_ref.shape[0], HD), jnp.bfloat16)


def fold(q_refs, keys_ref, wide_ref, scores_ref, rows, finish):
    each = q_refs[0].shape[0] // rows

    def scores(step):
        return lax.dot_general(
            q_refs[step // each][step % each * rows : (step % each + 1) * rows, :],
            keys_ref[...],
            (((1,), (1,)), ((), ())),
            preferred_element_type=jnp.float32,
        )

    count = len(q_refs) * each
    scores_ref[0] = scores(0)
    for step in range(count):
        if step + 1 < count:
            scores_ref[(step + 1) % 2] = scores(step + 1)
        tile = scores_ref[step % 2]
        top = jnp.max(tile, axis=1, keepdims=True)
        weights = jnp.exp2((tile - top) * SCALE).astype(jnp.bfloat16)
        sums = jnp.dot(weights, wide_ref[...], preferred_element_type=jnp.float32)
        finish(step, top, sums)


def first_kernel(
    q0_ref, q1_ref, q2_ref, q3_ref, kv_ref, top_ref, sums_ref, keys_ref, wide_ref, scores_ref, *, rows
):
    load_keys(kv_ref, keys_ref, wide_ref)

    def finish(step, top, sums):
        span = slice(step * rows, (step + 1) * rows)
        top_ref[span, :] = jnp.broadcast_to(top, (rows, HD))
        sums_ref[span, :] = sums

    fold((q0_ref, q1_ref, q2_ref, q3_ref), keys_ref, wide_ref, scores_ref, rows, finish)


def second_kernel(
    q0_ref,
    q1_ref,
    q2_ref,
    q3_ref,
    kv_ref,
    me_ref,
    top_ref,
    sums_ref,
    out_ref,
    keys_ref,
    wide_ref,
    scores_ref,
    *,
    rows,
):
    load_keys(kv_ref, keys_ref, wide_ref)
    blocks = rows // TOKENS
    each = HEADS // blocks
    lane = lax.broadcasted_iota(jnp.int32, (blocks, SIDE, HD), 2)

    def finish(step, own_top, own_sums):
        span = slice(step * rows, (step + 1) * rows)
        other_top = top_ref[span, :]
        top = jnp.maximum(own_top, other_top)
        own = jnp.exp2((own_top - top) * SCALE)
        other = jnp.exp2((other_top - top) * SCALE)
        total = own_sums[:, HD:] * own + sums_ref[span, HD:] * other
        share = (own_sums[:, :HD] * own + sums_ref[span, :HD] * other) / total
        rest = (jnp.log2(total) + top * SCALE).reshape(blocks, TOKENS, HD)
        side = jnp.zeros((blocks, SIDE, HD), jnp.float32)
        for term in range(3):
            piece = rest.astype(jnp.bfloat16).astype(jnp.float32)
            rest = rest - piece
            for group in range(TOKENS // SIDE):
                side = jnp.where(
                    lane == group * 3 + term, piece[:, group * SIDE : (group + 1) * SIDE, :], side
                )
        source = lax.rem(me_ref[0] + 4 - step // each, 4)
        out_ref[pl.ds(source * HEADS + step % each * blocks, blocks)] = jnp.concatenate(
            [share.reshape(blocks, TOKENS, HD), side], axis=1
        ).astype(jnp.bfloat16)

    fold((q0_ref, q1_ref, q2_ref, q3_ref), keys_ref, wide_ref, scores_ref, rows, finish)


def attend(queries, kv, me, state, rows=192):
    count, keys = 4 * queries[0].shape[0], kv.shape[0]
    specs = whole(5)
    if state is None:
        kernel, operands, name = first_kernel, (*queries, kv), "attend_first"
        out_shape = [
            jax.ShapeDtypeStruct((count, HD), jnp.float32),
            jax.ShapeDtypeStruct((count, 2 * HD), jnp.float32),
        ]
    else:
        kernel, operands, name = second_kernel, (*queries, kv, me, *state), "attend_second"
        specs = specs + [pl.BlockSpec(memory_space=pltpu.SMEM)] + whole(2)
        out_shape = [jax.ShapeDtypeStruct((count // TOKENS, TOKENS + SIDE, HD), jnp.bfloat16)]
    return pl.pallas_call(
        functools.partial(kernel, rows=rows),
        out_shape=out_shape,
        in_specs=specs,
        out_specs=whole(len(out_shape)),
        scratch_shapes=[
            pltpu.VMEM((keys, HD), jnp.bfloat16),
            pltpu.VMEM((keys, 2 * HD), jnp.bfloat16),
            pltpu.VMEM((2, rows, keys), jnp.float32),
        ],
        compiler_params=VMEM,
        cost_estimate=pl.CostEstimate(
            flops=(1 if state else 64) * 8 * count * keys * HD, bytes_accessed=4 << 20, transcendentals=count * keys
        ),
        name=name,
    )(*operands)


def combine_kernel(parts_ref, out_ref):
    for head in range(HEADS):
        blocks = [parts_ref[part * HEADS + head].astype(jnp.float32) for part in range(4)]
        merged = []
        for group in range(TOKENS // SIDE):
            rows = slice(group * SIDE, (group + 1) * SIDE)
            logs = []
            for block in blocks:
                side = block[TOKENS:, group * 3 : group * 3 + 3]
                logs.append(side[:, 0:1] + side[:, 1:2] + side[:, 2:3])
            top = jnp.maximum(jnp.maximum(logs[0], logs[1]), jnp.maximum(logs[2], logs[3]))
            factors = [jnp.exp2(log - top) for log in logs]
            total = (factors[0] + factors[1]) + (factors[2] + factors[3])
            acc = sum(blocks[part][rows] * (factors[part] / total) for part in range(4))
            merged.append(acc)
        out_ref[:, head * HD : (head + 1) * HD] = jnp.concatenate(merged, axis=0).astype(jnp.bfloat16)


def combine(parts):
    return pl.pallas_call(
        combine_kernel,
        out_shape=jax.ShapeDtypeStruct((TOKENS, HEADS * HD), jnp.bfloat16),
        in_specs=whole(1),
        out_specs=pl.BlockSpec(memory_space=pltpu.VMEM),
        compiler_params=VMEM,
        name="combine",
    )(parts)


def spread(array, axis, size):
    copies = jnp.broadcast_to(array[None], (size,) + array.shape)
    gathered = lax.all_to_all(copies, axis, split_axis=0, concat_axis=0, tiled=True)
    return gathered.reshape(size * array.shape[0], array.shape[1])


def per_device(queries, keys, values):
    packed = pack(queries, keys, values)
    mine = lax.all_to_all(packed, HEAD_GROUP, split_axis=0, concat_axis=0, tiled=True)
    mine = mine.reshape(HEADS * TOKENS, 3 * HD)
    own_q = mine[:, :HD]
    kv = spread(mine[:, HD:], "x", 4)
    shifts = [[(source, (source + by) % 4) for source in range(4)] for by in (1, 2, 3)]
    query = [own_q] + [lax.ppermute(own_q, "zh", pairs) for pairs in shifts]
    other_kv = lax.ppermute(kv, "c", [(0, 1), (1, 0)])
    me = lax.axis_index("zh").astype(jnp.int32).reshape(1)
    (parts,) = attend(query, other_kv, me, attend(query, kv, me, None))
    sent = lax.all_to_all(parts, BACK_GROUP, split_axis=0, concat_axis=0, tiled=True)
    return combine(sent)


def solution(mesh):
    fine = Mesh(mesh.devices.reshape(SIZES), AXES)
    placed = P(AXES, None)
    return jax.shard_map(
        per_device, mesh=fine, in_specs=(placed,) * 3, out_specs=placed, check_vma=False
    )
```

```python
import functools
import math

import jax
import jax.numpy as jnp
from jax import lax
from jax.experimental import pallas as pl
from jax.experimental.pallas import tpu as pltpu
from jax.sharding import Mesh, PartitionSpec as P

HD = 128
HEADS = 16
TOKENS = 24
SIDE = 8
LANES = 9
SCALE = math.log2(math.e) / math.sqrt(HD)
VMEM = pltpu.CompilerParams(vmem_limit_bytes=24 * 1024 * 1024)

AXES = ("yl", "c", "zh", "zl", "x", "yh")
SIZES = (4, 2, 4, 2, 4, 2)
HEAD_GROUP = ("yh", "yl", "zl")
BACK_GROUP = ("zh", "yh", "yl", "zl")


def whole(count):
    return [pl.BlockSpec(memory_space=pltpu.VMEM)] * count


def pack_kernel(q_ref, k_ref, v_ref, out_ref, near_ref, done):
    copies = [
        pltpu.make_async_copy(source, near_ref.at[place], done.at[place])
        for place, source in enumerate((q_ref, k_ref, v_ref))
    ]
    for copy in copies:
        copy.start()
    for place, copy in enumerate(copies):
        copy.wait()
        for head in range(HEADS):
            out_ref[head, :, place * HD : (place + 1) * HD] = near_ref[
                place, :, head * HD : (head + 1) * HD
            ]


def pack(queries, keys, values):
    return pl.pallas_call(
        pack_kernel,
        out_shape=jax.ShapeDtypeStruct((HEADS, TOKENS, 3 * HD), jnp.bfloat16),
        in_specs=[pl.BlockSpec(memory_space=pl.ANY)] * 3,
        out_specs=pl.BlockSpec(memory_space=pltpu.VMEM),
        scratch_shapes=[
            pltpu.VMEM((3, TOKENS, HEADS * HD), jnp.bfloat16),
            pltpu.SemaphoreType.DMA((3,)),
        ],
        name="pack",
    )(queries, keys, values)


def load_keys(kv_ref, keys_ref, wide_ref):
    keys_ref[...] = kv_ref[:, :HD]
    wide_ref[:, :HD] = kv_ref[:, HD:]
    wide_ref[:, HD:] = jnp.ones((kv_ref.shape[0], HD), jnp.bfloat16)


def fold(q_refs, keys_ref, wide_ref, scores_ref, rows, finish):
    each = q_refs[0].shape[0] // rows

    def scores(step):
        return lax.dot_general(
            q_refs[step // each][step % each * rows : (step % each + 1) * rows, :],
            keys_ref[...],
            (((1,), (1,)), ((), ())),
            preferred_element_type=jnp.float32,
        )

    count = len(q_refs) * each
    scores_ref[0] = scores(0)
    for step in range(count):
        if step + 1 < count:
            scores_ref[(step + 1) % 2] = scores(step + 1)
        tile = scores_ref[step % 2]
        top = jnp.max(tile, axis=1, keepdims=True)
        weights = jnp.exp2((tile - top) * SCALE).astype(jnp.bfloat16)
        sums = jnp.dot(weights, wide_ref[...], preferred_element_type=jnp.float32)
        finish(step, top, sums)


def first_kernel(
    q0_ref, q1_ref, q2_ref, q3_ref, kv_ref, top_ref, sums_ref, keys_ref, wide_ref, scores_ref, *, rows
):
    load_keys(kv_ref, keys_ref, wide_ref)

    def finish(step, top, sums):
        span = slice(step * rows, (step + 1) * rows)
        top_ref[span, :] = jnp.broadcast_to(top, (rows, HD))
        sums_ref[span, :] = sums

    fold((q0_ref, q1_ref, q2_ref, q3_ref), keys_ref, wide_ref, scores_ref, rows, finish)


def second_kernel(
    q0_ref,
    q1_ref,
    q2_ref,
    q3_ref,
    kv_ref,
    me_ref,
    top_ref,
    sums_ref,
    out_ref,
    keys_ref,
    wide_ref,
    scores_ref,
    *,
    rows,
):
    load_keys(kv_ref, keys_ref, wide_ref)
    blocks = rows // TOKENS
    each = HEADS // blocks
    lane = lax.broadcasted_iota(jnp.int32, (blocks, SIDE, HD), 2)

    def finish(step, own_top, own_sums):
        span = slice(step * rows, (step + 1) * rows)
        other_top = top_ref[span, :]
        top = jnp.maximum(own_top, other_top)
        own = jnp.exp2((own_top - top) * SCALE)
        other = jnp.exp2((other_top - top) * SCALE)
        total = own_sums[:, HD:] * own + sums_ref[span, HD:] * other
        share = (own_sums[:, :HD] * own + sums_ref[span, :HD] * other) / total
        rest = (jnp.log2(total) + top * SCALE).reshape(blocks, TOKENS, HD)
        side = jnp.zeros((blocks, SIDE, HD), jnp.float32)
        for term in range(3):
            piece = rest.astype(jnp.bfloat16).astype(jnp.float32)
            rest = rest - piece
            for group in range(TOKENS // SIDE):
                side = jnp.where(
                    lane == group * 3 + term, piece[:, group * SIDE : (group + 1) * SIDE, :], side
                )
        source = lax.rem(me_ref[0] + 4 - step // each, 4)
        out_ref[pl.ds(source * HEADS + step % each * blocks, blocks)] = jnp.concatenate(
            [share.reshape(blocks, TOKENS, HD), side], axis=1
        ).astype(jnp.bfloat16)

    fold((q0_ref, q1_ref, q2_ref, q3_ref), keys_ref, wide_ref, scores_ref, rows, finish)


def attend(queries, kv, me, state, rows=192):
    count, keys = 4 * queries[0].shape[0], kv.shape[0]
    specs = whole(5)
    if state is None:
        kernel, operands, name = first_kernel, (*queries, kv), "attend_first"
        out_shape = [
            jax.ShapeDtypeStruct((count, HD), jnp.float32),
            jax.ShapeDtypeStruct((count, 2 * HD), jnp.float32),
        ]
    else:
        kernel, operands, name = second_kernel, (*queries, kv, me, *state), "attend_second"
        specs = specs + [pl.BlockSpec(memory_space=pltpu.SMEM)] + whole(2)
        out_shape = [jax.ShapeDtypeStruct((count // TOKENS, TOKENS + SIDE, HD), jnp.bfloat16)]
    return pl.pallas_call(
        functools.partial(kernel, rows=rows),
        out_shape=out_shape,
        in_specs=specs,
        out_specs=whole(len(out_shape)),
        scratch_shapes=[
            pltpu.VMEM((keys, HD), jnp.bfloat16),
            pltpu.VMEM((keys, 2 * HD), jnp.bfloat16),
            pltpu.VMEM((2, rows, keys), jnp.float32),
        ],
        compiler_params=VMEM,
        cost_estimate=pl.CostEstimate(
            flops=(1 if state else 4) * 8 * count * keys * HD, bytes_accessed=4 << 20, transcendentals=count * keys
        ),
        name=name,
    )(*operands)


def combine_kernel(parts_ref, out_ref):
    for first in range(0, HEADS, SIDE):
        logs = []
        for part in range(4):
            side = 0.0
            for head in range(first, first + SIDE):
                tile = parts_ref[part * HEADS + head, TOKENS:, :].astype(jnp.float32)
                if head > first:
                    tile = pltpu.roll(tile, (head - first) * LANES, 1)
                side = side + tile
            logs.append(side + pltpu.roll(side, HD - 1, 1) + pltpu.roll(side, HD - 2, 1))
        top = jnp.maximum(jnp.maximum(logs[0], logs[1]), jnp.maximum(logs[2], logs[3]))
        factors = [jnp.exp2(log - top) for log in logs]
        total = (factors[0] + factors[1]) + (factors[2] + factors[3])
        factors = [factor / total for factor in factors]
        for head in range(first, first + SIDE):
            merged = 0.0
            for part in range(4):
                weights = []
                for group in range(TOKENS // SIDE):
                    lane = (head - first) * LANES + 3 * group
                    weight = factors[part][:, lane : lane + 1]
                    weights.append(jnp.broadcast_to(weight, (SIDE, HD)))
                rows = parts_ref[part * HEADS + head, :TOKENS, :].astype(jnp.float32)
                merged = merged + rows * jnp.concatenate(weights, axis=0)
            out_ref[:, head * HD : (head + 1) * HD] = merged.astype(jnp.bfloat16)


def combine(parts):
    return pl.pallas_call(
        combine_kernel,
        out_shape=jax.ShapeDtypeStruct((TOKENS, HEADS * HD), jnp.bfloat16),
        in_specs=whole(1),
        out_specs=pl.BlockSpec(memory_space=pltpu.VMEM),
        compiler_params=VMEM,
        name="combine",
    )(parts)


def spread(array, axis, size):
    copies = jnp.broadcast_to(array[None], (size,) + array.shape)
    gathered = lax.all_to_all(copies, axis, split_axis=0, concat_axis=0, tiled=True)
    return gathered.reshape(size * array.shape[0], array.shape[1])


def per_device(queries, keys, values):
    packed = pack(queries, keys, values)
    mine = lax.all_to_all(packed, HEAD_GROUP, split_axis=0, concat_axis=0, tiled=True)
    mine = mine.reshape(HEADS * TOKENS, 3 * HD)
    own_q = mine[:, :HD]
    kv = spread(mine[:, HD:], "x", 4)
    shifts = [[(source, (source + by) % 4) for source in range(4)] for by in (1, 2, 3)]
    query = [own_q] + [lax.ppermute(own_q, "zh", pairs) for pairs in shifts]
    other_kv = lax.ppermute(kv, "c", [(0, 1), (1, 0)])
    me = lax.axis_index("zh").astype(jnp.int32).reshape(1)
    (parts,) = attend(query, other_kv, me, attend(query, kv, me, None))
    sent = lax.all_to_all(parts, BACK_GROUP, split_axis=0, concat_axis=0, tiled=True)
    return combine(sent)


def solution(mesh):
    fine = Mesh(mesh.devices.reshape(SIZES), AXES)
    placed = P(AXES, None)
    return jax.shard_map(
        per_device, mesh=fine, in_specs=(placed,) * 3, out_specs=placed, check_vma=False
    )
```

```python
import functools
import math

import jax
import jax.numpy as jnp
from jax import lax
from jax.experimental import pallas as pl
from jax.experimental.pallas import tpu as pltpu
from jax.sharding import Mesh, PartitionSpec as P

HD = 128
HEADS = 16
TOKENS = 24
SIDE = 8
LANES = 9
TURNS = (0, 1, 3, 2)
FIRST = 64
SCALE = math.log2(math.e) / math.sqrt(HD)
VMEM = pltpu.CompilerParams(vmem_limit_bytes=24 * 1024 * 1024)

AXES = ("yl", "c", "zh", "zl", "x", "yh")
SIZES = (4, 2, 4, 2, 4, 2)
HEAD_GROUP = ("yh", "yl", "zl")
BACK_GROUP = ("zh", "yh", "yl", "zl")


def whole(count):
    return [pl.BlockSpec(memory_space=pltpu.VMEM)] * count


def pack_kernel(q_ref, k_ref, v_ref, out_ref, near_ref, done):
    copies = [
        pltpu.make_async_copy(source, near_ref.at[place], done.at[place])
        for place, source in enumerate((q_ref, k_ref, v_ref))
    ]
    for copy in copies:
        copy.start()
    for place, copy in enumerate(copies):
        copy.wait()
        for head in range(HEADS):
            out_ref[head, :, place * HD : (place + 1) * HD] = near_ref[
                place, :, head * HD : (head + 1) * HD
            ]


def pack(queries, keys, values):
    return pl.pallas_call(
        pack_kernel,
        out_shape=jax.ShapeDtypeStruct((HEADS, TOKENS, 3 * HD), jnp.bfloat16),
        in_specs=[pl.BlockSpec(memory_space=pl.ANY)] * 3,
        out_specs=pl.BlockSpec(memory_space=pltpu.VMEM),
        scratch_shapes=[
            pltpu.VMEM((3, TOKENS, HEADS * HD), jnp.bfloat16),
            pltpu.SemaphoreType.DMA((3,)),
        ],
        name="pack",
    )(queries, keys, values)


def load_keys(kv_ref, keys_ref, wide_ref):
    keys_ref[...] = kv_ref[:, :HD]
    wide_ref[:, :HD] = kv_ref[:, HD:]
    wide_ref[:, HD:] = jnp.ones((kv_ref.shape[0], HD), jnp.bfloat16)


def fold(q_refs, keys_ref, wide_ref, scores_ref, rows, finish):
    each = q_refs[0].shape[0] // rows

    def scores(step):
        return lax.dot_general(
            q_refs[step // each][step % each * rows : (step % each + 1) * rows, :],
            keys_ref[...],
            (((1,), (1,)), ((), ())),
            preferred_element_type=jnp.float32,
        )

    count = len(q_refs) * each
    scores_ref[0] = scores(0)
    for step in range(count):
        if step + 1 < count:
            scores_ref[(step + 1) % 2] = scores(step + 1)
        tile = scores_ref[step % 2]
        top = jnp.max(tile, axis=1, keepdims=True)
        weights = jnp.exp2((tile - top) * SCALE).astype(jnp.bfloat16)
        sums = jnp.dot(weights, wide_ref[...], preferred_element_type=jnp.float32)
        finish(step, top, sums)


def store_state(top_ref, sums_ref, rows):
    def finish(step, top, sums):
        span = slice(step * rows, (step + 1) * rows)
        top_ref[span, :] = jnp.broadcast_to(top, (rows, HD))
        sums_ref[span, :] = sums

    return finish


def first_kernel(
    q0_ref, q1_ref, q2_ref, kv_ref, top_ref, sums_ref, keys_ref, wide_ref, scores_ref, *, rows
):
    load_keys(kv_ref, keys_ref, wide_ref)
    q_refs = (q0_ref, q1_ref, q2_ref)
    fold(q_refs, keys_ref, wide_ref, scores_ref, rows, store_state(top_ref, sums_ref, rows))


def second_kernel(
    q0_ref,
    q1_ref,
    q2_ref,
    q3_ref,
    kv_ref,
    other_ref,
    me_ref,
    top_ref,
    sums_ref,
    out_ref,
    keys_ref,
    wide_ref,
    scores_ref,
    other_keys_ref,
    other_wide_ref,
    last_top_ref,
    last_sums_ref,
    *,
    rows,
):
    load_keys(kv_ref, keys_ref, wide_ref)
    load_keys(other_ref, other_keys_ref, other_wide_ref)
    last = store_state(last_top_ref, last_sums_ref, rows)
    fold((q3_ref,), keys_ref, wide_ref, scores_ref, rows, last)
    blocks = rows // TOKENS
    each = HEADS // blocks
    lane = lax.broadcasted_iota(jnp.int32, (blocks, SIDE, HD), 2)

    def finish(step, own_top, own_sums):
        done = step if step < 3 * each else step - 3 * each
        span = slice(done * rows, (done + 1) * rows)
        before_top = (top_ref if step < 3 * each else last_top_ref)[span, :]
        before_sums = (sums_ref if step < 3 * each else last_sums_ref)[span, :]
        top = jnp.maximum(own_top, before_top)
        own = jnp.exp2((own_top - top) * SCALE)
        before = jnp.exp2((before_top - top) * SCALE)
        total = own_sums[:, HD:] * own + before_sums[:, HD:] * before
        share = (own_sums[:, :HD] * own + before_sums[:, :HD] * before) / total
        rest = (jnp.log2(total) + top * SCALE).reshape(blocks, TOKENS, HD)
        side = jnp.zeros((blocks, SIDE, HD), jnp.float32)
        for term in range(3):
            piece = rest.astype(jnp.bfloat16).astype(jnp.float32)
            rest = rest - piece
            for group in range(TOKENS // SIDE):
                side = jnp.where(
                    lane == group * 3 + term, piece[:, group * SIDE : (group + 1) * SIDE, :], side
                )
        source = me_ref[0] ^ TURNS[step // each]
        out_ref[pl.ds(source * HEADS + step % each * blocks, blocks)] = jnp.concatenate(
            [share.reshape(blocks, TOKENS, HD), side], axis=1
        ).astype(jnp.bfloat16)

    q_refs = (q0_ref, q1_ref, q2_ref, q3_ref)
    fold(q_refs, other_keys_ref, other_wide_ref, scores_ref, rows, finish)


def attend(queries, kv, other_kv, me, rows=192):
    slot, keys = queries[0].shape[0], kv.shape[0]
    scratch = [
        pltpu.VMEM((keys, HD), jnp.bfloat16),
        pltpu.VMEM((keys, 2 * HD), jnp.bfloat16),
        pltpu.VMEM((2, rows, keys), jnp.float32),
    ]
    state = pl.pallas_call(
        functools.partial(first_kernel, rows=rows),
        out_shape=[
            jax.ShapeDtypeStruct((3 * slot, HD), jnp.float32),
            jax.ShapeDtypeStruct((3 * slot, 2 * HD), jnp.float32),
        ],
        in_specs=whole(4),
        out_specs=whole(2),
        scratch_shapes=scratch,
        compiler_params=VMEM,
        cost_estimate=pl.CostEstimate(
            flops=FIRST * 3 * slot * keys * HD, bytes_accessed=4 << 20, transcendentals=3 * slot * keys
        ),
        name="attend_first",
    )(*queries[:3], kv)
    return pl.pallas_call(
        functools.partial(second_kernel, rows=rows),
        out_shape=jax.ShapeDtypeStruct((4 * slot // TOKENS, TOKENS + SIDE, HD), jnp.bfloat16),
        in_specs=whole(6) + [pl.BlockSpec(memory_space=pltpu.SMEM)] + whole(2),
        out_specs=pl.BlockSpec(memory_space=pltpu.VMEM),
        scratch_shapes=scratch
        + scratch[:2]
        + [pltpu.VMEM((slot, HD), jnp.float32), pltpu.VMEM((slot, 2 * HD), jnp.float32)],
        compiler_params=VMEM,
        cost_estimate=pl.CostEstimate(
            flops=8 * 5 * slot * keys * HD, bytes_accessed=4 << 20, transcendentals=5 * slot * keys
        ),
        name="attend_second",
    )(*queries, kv, other_kv, me, *state)


def combine_kernel(parts_ref, out_ref):
    for first in range(0, HEADS, SIDE):
        logs = []
        for part in range(4):
            side = 0.0
            for head in range(first, first + SIDE):
                tile = parts_ref[part * HEADS + head, TOKENS:, :].astype(jnp.float32)
                if head > first:
                    tile = pltpu.roll(tile, (head - first) * LANES, 1)
                side = side + tile
            logs.append(side + pltpu.roll(side, HD - 1, 1) + pltpu.roll(side, HD - 2, 1))
        top = jnp.maximum(jnp.maximum(logs[0], logs[1]), jnp.maximum(logs[2], logs[3]))
        factors = [jnp.exp2(log - top) for log in logs]
        total = (factors[0] + factors[1]) + (factors[2] + factors[3])
        factors = [factor / total for factor in factors]
        for head in range(first, first + SIDE):
            merged = 0.0
            for part in range(4):
                weights = []
                for group in range(TOKENS // SIDE):
                    lane = (head - first) * LANES + 3 * group
                    weight = factors[part][:, lane : lane + 1]
                    weights.append(jnp.broadcast_to(weight, (SIDE, HD)))
                rows = parts_ref[part * HEADS + head, :TOKENS, :].astype(jnp.float32)
                merged = merged + rows * jnp.concatenate(weights, axis=0)
            out_ref[:, head * HD : (head + 1) * HD] = merged.astype(jnp.bfloat16)


def combine(parts):
    return pl.pallas_call(
        combine_kernel,
        out_shape=jax.ShapeDtypeStruct((TOKENS, HEADS * HD), jnp.bfloat16),
        in_specs=whole(1),
        out_specs=pl.BlockSpec(memory_space=pltpu.VMEM),
        compiler_params=VMEM,
        name="combine",
    )(parts)


def spread(array, axis, size):
    copies = jnp.broadcast_to(array[None], (size,) + array.shape)
    gathered = lax.all_to_all(copies, axis, split_axis=0, concat_axis=0, tiled=True)
    return gathered.reshape(size * array.shape[0], array.shape[1])


def swap(by):
    return [(source, source ^ by) for source in range(4)]


def per_device(queries, keys, values):
    packed = pack(queries, keys, values)
    mine = lax.all_to_all(packed, HEAD_GROUP, split_axis=0, concat_axis=0, tiled=True)
    mine = mine.reshape(HEADS * TOKENS, 3 * HD)
    own_q = mine[:, :HD]
    kv = spread(mine[:, HD:], "x", 4)
    query = [own_q] + [lax.ppermute(own_q, "zh", swap(by)) for by in TURNS[1:]]
    other_kv = lax.ppermute(kv, "c", [(0, 1), (1, 0)])
    me = lax.axis_index("zh").astype(jnp.int32).reshape(1)
    parts = attend(query, kv, other_kv, me)
    sent = lax.all_to_all(parts, BACK_GROUP, split_axis=0, concat_axis=0, tiled=True)
    return combine(sent)


def solution(mesh):
    fine = Mesh(mesh.devices.reshape(SIZES), AXES)
    placed = P(AXES, None)
    return jax.shard_map(
        per_device, mesh=fine, in_specs=(placed,) * 3, out_specs=placed, check_vma=False
    )
```

```python
import functools
import math

import jax
import jax.numpy as jnp
from jax import lax
from jax.experimental import pallas as pl
from jax.experimental.pallas import tpu as pltpu
from jax.sharding import Mesh, PartitionSpec as P

HD = 128
HEADS = 16
TOKENS = 24
SIDE = 8
LANES = 9
TURNS = (0, 1, 3, 2)
FIRST = 64
SCALE = math.log2(math.e) / math.sqrt(HD)
VMEM = pltpu.CompilerParams(vmem_limit_bytes=24 * 1024 * 1024)

AXES = ("yl", "c", "zh", "zl", "x", "yh")
SIZES = (4, 2, 4, 2, 4, 2)
HEAD_GROUP = ("yh", "yl", "zl")
BACK_GROUP = ("zh", "yh", "yl", "zl")


def whole(count):
    return [pl.BlockSpec(memory_space=pltpu.VMEM)] * count


def pack_kernel(q_ref, k_ref, v_ref, out_ref, near_ref, ready_ref, done):
    copies = [
        pltpu.make_async_copy(source, near_ref.at[place], done.at[place])
        for place, source in enumerate((q_ref, k_ref, v_ref))
    ]
    for copy in copies:
        copy.start()
    sent = []
    for place, copy in enumerate(copies):
        copy.wait()
        lanes = slice(place * HD, (place + 1) * HD)
        for head in range(HEADS):
            ready_ref[head, :, lanes] = near_ref[place, :, head * HD : (head + 1) * HD]
        sent.append(
            pltpu.make_async_copy(
                ready_ref.at[:, :, lanes], out_ref.at[:, :, lanes], done.at[3 + place]
            )
        )
        sent[-1].start()
    for copy in sent:
        copy.wait()


def pack(queries, keys, values):
    return pl.pallas_call(
        pack_kernel,
        out_shape=jax.ShapeDtypeStruct((HEADS, TOKENS, 3 * HD), jnp.bfloat16),
        in_specs=[pl.BlockSpec(memory_space=pl.ANY)] * 3,
        out_specs=pl.BlockSpec(memory_space=pl.ANY),
        scratch_shapes=[
            pltpu.VMEM((3, TOKENS, HEADS * HD), jnp.bfloat16),
            pltpu.VMEM((HEADS, TOKENS, 3 * HD), jnp.bfloat16),
            pltpu.SemaphoreType.DMA((6,)),
        ],
        name="pack",
    )(queries, keys, values)


def load_values(kv_ref, wide_ref):
    wide_ref[:, :HD] = kv_ref[:, HD:]
    wide_ref[:, HD:] = jnp.ones((kv_ref.shape[0], HD), jnp.bfloat16)


def fold(q_refs, kv_ref, wide_ref, scores_ref, rows, finish):
    each = q_refs[0].shape[0] // rows

    def scores(step):
        return lax.dot_general(
            q_refs[step // each][step % each * rows : (step % each + 1) * rows, :],
            kv_ref[:, :HD],
            (((1,), (1,)), ((), ())),
            preferred_element_type=jnp.float32,
        )

    count = len(q_refs) * each
    scores_ref[0] = scores(0)
    for step in range(count):
        if step + 1 < count:
            scores_ref[(step + 1) % 2] = scores(step + 1)
        tile = scores_ref[step % 2]
        top = jnp.max(tile, axis=1, keepdims=True)
        weights = jnp.exp2((tile - top) * SCALE).astype(jnp.bfloat16)
        sums = jnp.dot(weights, wide_ref[...], preferred_element_type=jnp.float32)
        finish(step, top, sums)


def store_state(top_ref, sums_ref, rows):
    def finish(step, top, sums):
        span = slice(step * rows, (step + 1) * rows)
        top_ref[span, :] = jnp.broadcast_to(top, (rows, HD))
        sums_ref[span, :] = sums

    return finish


def first_kernel(
    q0_ref, q1_ref, q2_ref, kv_ref, top_ref, sums_ref, wide_ref, scores_ref, *, rows
):
    load_values(kv_ref, wide_ref)
    q_refs = (q0_ref, q1_ref, q2_ref)
    fold(q_refs, kv_ref, wide_ref, scores_ref, rows, store_state(top_ref, sums_ref, rows))


def second_kernel(
    q0_ref,
    q1_ref,
    q2_ref,
    q3_ref,
    kv_ref,
    other_ref,
    me_ref,
    top_ref,
    sums_ref,
    out_ref,
    wide_ref,
    scores_ref,
    other_wide_ref,
    last_top_ref,
    last_sums_ref,
    *,
    rows,
):
    load_values(kv_ref, wide_ref)
    load_values(other_ref, other_wide_ref)
    last = store_state(last_top_ref, last_sums_ref, rows)
    fold((q3_ref,), kv_ref, wide_ref, scores_ref, rows, last)
    blocks = rows // TOKENS
    each = HEADS // blocks
    lane = lax.broadcasted_iota(jnp.int32, (blocks, SIDE, HD), 2)

    def finish(step, own_top, own_sums):
        done = step if step < 3 * each else step - 3 * each
        span = slice(done * rows, (done + 1) * rows)
        before_top = (top_ref if step < 3 * each else last_top_ref)[span, :]
        before_sums = (sums_ref if step < 3 * each else last_sums_ref)[span, :]
        top = jnp.maximum(own_top, before_top)
        own = jnp.exp2((own_top - top) * SCALE)
        before = jnp.exp2((before_top - top) * SCALE)
        total = own_sums[:, HD:] * own + before_sums[:, HD:] * before
        share = (own_sums[:, :HD] * own + before_sums[:, :HD] * before) / total
        rest = (jnp.log2(total) + top * SCALE).reshape(blocks, TOKENS, HD)
        side = jnp.zeros((blocks, SIDE, HD), jnp.float32)
        for term in range(3):
            piece = rest.astype(jnp.bfloat16).astype(jnp.float32)
            rest = rest - piece
            for group in range(TOKENS // SIDE):
                side = jnp.where(
                    lane == group * 3 + term, piece[:, group * SIDE : (group + 1) * SIDE, :], side
                )
        source = me_ref[0] ^ TURNS[step // each]
        out_ref[pl.ds(source * HEADS + step % each * blocks, blocks)] = jnp.concatenate(
            [share.reshape(blocks, TOKENS, HD), side], axis=1
        ).astype(jnp.bfloat16)

    q_refs = (q0_ref, q1_ref, q2_ref, q3_ref)
    fold(q_refs, other_ref, other_wide_ref, scores_ref, rows, finish)


def attend(queries, kv, other_kv, me, rows=192):
    slot, keys = queries[0].shape[0], kv.shape[0]
    scratch = [
        pltpu.VMEM((keys, 2 * HD), jnp.bfloat16),
        pltpu.VMEM((2, rows, keys), jnp.float32),
    ]
    state = pl.pallas_call(
        functools.partial(first_kernel, rows=rows),
        out_shape=[
            jax.ShapeDtypeStruct((3 * slot, HD), jnp.float32),
            jax.ShapeDtypeStruct((3 * slot, 2 * HD), jnp.float32),
        ],
        in_specs=whole(4),
        out_specs=whole(2),
        scratch_shapes=scratch,
        compiler_params=VMEM,
        cost_estimate=pl.CostEstimate(
            flops=FIRST * 3 * slot * keys * HD, bytes_accessed=4 << 20, transcendentals=3 * slot * keys
        ),
        name="attend_first",
    )(*queries[:3], kv)
    return pl.pallas_call(
        functools.partial(second_kernel, rows=rows),
        out_shape=jax.ShapeDtypeStruct((4 * slot // TOKENS, TOKENS + SIDE, HD), jnp.bfloat16),
        in_specs=whole(6) + [pl.BlockSpec(memory_space=pltpu.SMEM)] + whole(2),
        out_specs=pl.BlockSpec(memory_space=pltpu.VMEM),
        scratch_shapes=scratch
        + scratch[:1]
        + [pltpu.VMEM((slot, HD), jnp.float32), pltpu.VMEM((slot, 2 * HD), jnp.float32)],
        compiler_params=VMEM,
        cost_estimate=pl.CostEstimate(
            flops=8 * 5 * slot * keys * HD, bytes_accessed=4 << 20, transcendentals=5 * slot * keys
        ),
        name="attend_second",
    )(*queries, kv, other_kv, me, *state)


def combine_kernel(parts_ref, out_ref):
    for first in range(0, HEADS, SIDE):
        logs = []
        for part in range(4):
            side = 0.0
            for head in range(first, first + SIDE):
                tile = parts_ref[part * HEADS + head, TOKENS:, :].astype(jnp.float32)
                if head > first:
                    tile = pltpu.roll(tile, (head - first) * LANES, 1)
                side = side + tile
            logs.append(side + pltpu.roll(side, HD - 1, 1) + pltpu.roll(side, HD - 2, 1))
        top = jnp.maximum(jnp.maximum(logs[0], logs[1]), jnp.maximum(logs[2], logs[3]))
        factors = [jnp.exp2(log - top) for log in logs]
        total = (factors[0] + factors[1]) + (factors[2] + factors[3])
        factors = [factor / total for factor in factors]
        for head in range(first, first + SIDE):
            merged = 0.0
            for part in range(4):
                weights = []
                for group in range(TOKENS // SIDE):
                    lane = (head - first) * LANES + 3 * group
                    weight = factors[part][:, lane : lane + 1]
                    weights.append(jnp.broadcast_to(weight, (SIDE, HD)))
                rows = parts_ref[part * HEADS + head, :TOKENS, :].astype(jnp.float32)
                merged = merged + rows * jnp.concatenate(weights, axis=0)
            out_ref[:, head * HD : (head + 1) * HD] = merged.astype(jnp.bfloat16)


def combine(parts):
    return pl.pallas_call(
        combine_kernel,
        out_shape=jax.ShapeDtypeStruct((TOKENS, HEADS * HD), jnp.bfloat16),
        in_specs=whole(1),
        out_specs=pl.BlockSpec(memory_space=pltpu.VMEM),
        compiler_params=VMEM,
        name="combine",
    )(parts)


def spread(array, axis, size):
    copies = jnp.broadcast_to(array[None], (size,) + array.shape)
    gathered = lax.all_to_all(copies, axis, split_axis=0, concat_axis=0, tiled=True)
    return gathered.reshape(size * array.shape[0], array.shape[1])


def swap(by):
    return [(source, source ^ by) for source in range(4)]


def per_device(queries, keys, values):
    packed = pack(queries, keys, values)
    mine = lax.all_to_all(packed, HEAD_GROUP, split_axis=0, concat_axis=0, tiled=True)
    mine = mine.reshape(HEADS * TOKENS, 3 * HD)
    own_q = mine[:, :HD]
    kv = spread(mine[:, HD:], "x", 4)
    query = [own_q] + [lax.ppermute(own_q, "zh", swap(by)) for by in TURNS[1:]]
    other_kv = lax.ppermute(kv, "c", [(0, 1), (1, 0)])
    me = lax.axis_index("zh").astype(jnp.int32).reshape(1)
    parts = attend(query, kv, other_kv, me)
    sent = lax.all_to_all(parts, BACK_GROUP, split_axis=0, concat_axis=0, tiled=True)
    return combine(sent)


def solution(mesh):
    fine = Mesh(mesh.devices.reshape(SIZES), AXES)
    placed = P(AXES, None)
    return jax.shard_map(
        per_device, mesh=fine, in_specs=(placed,) * 3, out_specs=placed, check_vma=False
    )
```

```python
import functools
import math

import jax
import jax.numpy as jnp
from jax import lax
from jax.experimental import pallas as pl
from jax.experimental.pallas import tpu as pltpu
from jax.sharding import Mesh, PartitionSpec as P

HD = 128
HEADS = 16
TOKENS = 24
SIDE = 8
LANES = 9
TURNS = (0, 1, 3, 2)
FIRST = 64
SCALE = math.log2(math.e) / math.sqrt(HD)
VMEM = pltpu.CompilerParams(vmem_limit_bytes=24 * 1024 * 1024)

AXES = ("yl", "c", "zh", "zl", "x", "yh")
SIZES = (4, 2, 4, 2, 4, 2)
HEAD_GROUP = ("yh", "yl", "zl")
BACK_GROUP = ("zh", "yh", "yl", "zl")


def whole(count):
    return [pl.BlockSpec(memory_space=pltpu.VMEM)] * count


def pack_kernel(q_ref, k_ref, v_ref, out_ref, near_ref, ready_ref, done):
    copies = [
        pltpu.make_async_copy(source, near_ref.at[place], done.at[place])
        for place, source in enumerate((q_ref, k_ref, v_ref))
    ]
    for copy in copies:
        copy.start()
    sent = []
    for place, copy in enumerate(copies):
        copy.wait()
        lanes = slice(place * HD, (place + 1) * HD)
        for head in range(HEADS):
            ready_ref[head, :, lanes] = near_ref[place, :, head * HD : (head + 1) * HD]
        sent.append(
            pltpu.make_async_copy(
                ready_ref.at[:, :, lanes], out_ref.at[:, :, lanes], done.at[3 + place]
            )
        )
        sent[-1].start()
    for copy in sent:
        copy.wait()


def pack(queries, keys, values):
    return pl.pallas_call(
        pack_kernel,
        out_shape=jax.ShapeDtypeStruct((HEADS, TOKENS, 3 * HD), jnp.bfloat16),
        in_specs=[pl.BlockSpec(memory_space=pl.ANY)] * 3,
        out_specs=pl.BlockSpec(memory_space=pl.ANY),
        scratch_shapes=[
            pltpu.VMEM((3, TOKENS, HEADS * HD), jnp.bfloat16),
            pltpu.VMEM((HEADS, TOKENS, 3 * HD), jnp.bfloat16),
            pltpu.SemaphoreType.DMA((6,)),
        ],
        name="pack",
    )(queries, keys, values)


def load_values(kv_ref, wide_ref):
    wide_ref[:, :HD] = kv_ref[:, HD:]
    wide_ref[:, HD:] = jnp.ones((kv_ref.shape[0], HD), jnp.bfloat16)


def fold(q_refs, kv_ref, wide_ref, scores_ref, rows, finish):
    each = q_refs[0].shape[0] // rows

    def scores(step):
        return lax.dot_general(
            q_refs[step // each][step % each * rows : (step % each + 1) * rows, :],
            kv_ref[:, :HD],
            (((1,), (1,)), ((), ())),
            preferred_element_type=jnp.float32,
        )

    count = len(q_refs) * each
    scores_ref[0] = scores(0)
    for step in range(count):
        if step + 1 < count:
            scores_ref[(step + 1) % 2] = scores(step + 1)
        tile = scores_ref[step % 2]
        top = jnp.max(tile, axis=1, keepdims=True)
        weights = jnp.exp2((tile - top) * SCALE).astype(jnp.bfloat16)
        sums = jnp.dot(weights, wide_ref[...], preferred_element_type=jnp.float32)
        finish(step, top, sums)


def store_state(top_ref, sums_ref, rows):
    def finish(step, top, sums):
        span = slice(step * rows, (step + 1) * rows)
        top_ref[span, :] = jnp.broadcast_to(top, (rows, HD))
        sums_ref[span, :] = sums

    return finish


def first_kernel(
    q0_ref, q1_ref, q2_ref, kv_ref, top_ref, sums_ref, wide_ref, scores_ref, *, rows
):
    load_values(kv_ref, wide_ref)
    q_refs = (q0_ref, q1_ref, q2_ref)
    fold(q_refs, kv_ref, wide_ref, scores_ref, rows, store_state(top_ref, sums_ref, rows))


def second_kernel(
    q0_ref,
    q1_ref,
    q2_ref,
    q3_ref,
    kv_ref,
    other_ref,
    me_ref,
    top_ref,
    sums_ref,
    out_ref,
    wide_ref,
    scores_ref,
    other_wide_ref,
    last_top_ref,
    last_sums_ref,
    *,
    rows,
):
    load_values(kv_ref, wide_ref)
    load_values(other_ref, other_wide_ref)
    last = store_state(last_top_ref, last_sums_ref, rows)
    fold((q3_ref,), kv_ref, wide_ref, scores_ref, rows, last)
    blocks = rows // TOKENS
    each = HEADS // blocks
    lane = lax.broadcasted_iota(jnp.int32, (blocks, SIDE, HD), 2)

    def finish(step, own_top, own_sums):
        done = step if step < 3 * each else step - 3 * each
        span = slice(done * rows, (done + 1) * rows)
        before_top = (top_ref if step < 3 * each else last_top_ref)[span, :]
        before_sums = (sums_ref if step < 3 * each else last_sums_ref)[span, :]
        top = jnp.maximum(own_top, before_top)
        own = jnp.exp2((own_top - top) * SCALE)
        before = jnp.exp2((before_top - top) * SCALE)
        total = own_sums[:, HD:] * own + before_sums[:, HD:] * before
        share = (own_sums[:, :HD] * own + before_sums[:, :HD] * before) / total
        rest = (jnp.log2(total) + top * SCALE).reshape(blocks, TOKENS, HD)
        side = jnp.zeros((blocks, SIDE, HD), jnp.float32)
        for term in range(3):
            piece = rest.astype(jnp.bfloat16).astype(jnp.float32)
            rest = rest - piece
            for group in range(TOKENS // SIDE):
                side = jnp.where(
                    lane == group * 3 + term, piece[:, group * SIDE : (group + 1) * SIDE, :], side
                )
        source = me_ref[0] ^ TURNS[step // each]
        out_ref[pl.ds(source * HEADS + step % each * blocks, blocks)] = jnp.concatenate(
            [share.reshape(blocks, TOKENS, HD), side], axis=1
        ).astype(jnp.bfloat16)

    q_refs = (q0_ref, q1_ref, q2_ref, q3_ref)
    fold(q_refs, other_ref, other_wide_ref, scores_ref, rows, finish)


def attend(queries, kv, other_kv, me, rows=192):
    slot, keys = queries[0].shape[0], kv.shape[0]
    scratch = [
        pltpu.VMEM((keys, 2 * HD), jnp.bfloat16),
        pltpu.VMEM((2, rows, keys), jnp.float32),
    ]
    state = pl.pallas_call(
        functools.partial(first_kernel, rows=rows),
        out_shape=[
            jax.ShapeDtypeStruct((3 * slot, HD), jnp.float32),
            jax.ShapeDtypeStruct((3 * slot, 2 * HD), jnp.float32),
        ],
        in_specs=whole(4),
        out_specs=whole(2),
        scratch_shapes=scratch,
        compiler_params=VMEM,
        cost_estimate=pl.CostEstimate(
            flops=FIRST * 3 * slot * keys * HD, bytes_accessed=4 << 20, transcendentals=3 * slot * keys
        ),
        name="attend_first",
    )(*queries[:3], kv)
    return pl.pallas_call(
        functools.partial(second_kernel, rows=rows),
        out_shape=jax.ShapeDtypeStruct((4 * slot // TOKENS, TOKENS + SIDE, HD), jnp.bfloat16),
        in_specs=whole(6) + [pl.BlockSpec(memory_space=pltpu.SMEM)] + whole(2),
        out_specs=pl.BlockSpec(memory_space=pltpu.VMEM),
        scratch_shapes=scratch
        + scratch[:1]
        + [pltpu.VMEM((slot, HD), jnp.float32), pltpu.VMEM((slot, 2 * HD), jnp.float32)],
        compiler_params=VMEM,
        cost_estimate=pl.CostEstimate(
            flops=8 * 5 * slot * keys * HD, bytes_accessed=4 << 20, transcendentals=5 * slot * keys
        ),
        name="attend_second",
    )(*queries, kv, other_kv, me, *state)


def combine_kernel(parts_ref, out_ref):
    for first in range(0, HEADS, SIDE):
        logs = []
        for part in range(4):
            side = 0.0
            for head in range(first, first + SIDE):
                tile = parts_ref[part * HEADS + head, TOKENS:, :].astype(jnp.float32)
                if head > first:
                    tile = pltpu.roll(tile, (head - first) * LANES, 1)
                side = side + tile
            logs.append(side + pltpu.roll(side, HD - 1, 1) + pltpu.roll(side, HD - 2, 1))
        top = jnp.maximum(jnp.maximum(logs[0], logs[1]), jnp.maximum(logs[2], logs[3]))
        factors = [jnp.exp2(log - top) for log in logs]
        total = (factors[0] + factors[1]) + (factors[2] + factors[3])
        factors = [factor / total for factor in factors]
        for head in range(first, first + SIDE):
            merged = 0.0
            for part in range(4):
                weights = []
                for group in range(TOKENS // SIDE):
                    lane = (head - first) * LANES + 3 * group
                    weight = factors[part][:, lane : lane + 1]
                    weights.append(jnp.broadcast_to(weight, (SIDE, HD)))
                rows = parts_ref[part * HEADS + head, :TOKENS, :].astype(jnp.float32)
                merged = merged + rows * jnp.concatenate(weights, axis=0)
            out_ref[:, head * HD : (head + 1) * HD] = merged.astype(jnp.bfloat16)


def combine(parts):
    return pl.pallas_call(
        combine_kernel,
        out_shape=jax.ShapeDtypeStruct((TOKENS, HEADS * HD), jnp.bfloat16),
        in_specs=whole(1),
        out_specs=pl.BlockSpec(memory_space=pltpu.VMEM),
        compiler_params=VMEM,
        name="combine",
    )(parts)


def copies_kernel(in_ref, out_ref, done):
    copies = [
        pltpu.make_async_copy(in_ref.at[:, HD:], out_ref.at[member], done.at[member])
        for member in range(4)
    ]
    for copy in copies:
        copy.start()
    for copy in copies:
        copy.wait()


def spread(mine):
    copies = pl.pallas_call(
        copies_kernel,
        out_shape=jax.ShapeDtypeStruct((4, mine.shape[0], 2 * HD), jnp.bfloat16),
        in_specs=whole(1),
        out_specs=pl.BlockSpec(memory_space=pl.ANY),
        scratch_shapes=[pltpu.SemaphoreType.DMA((4,))],
        compiler_params=VMEM,
        name="copies",
    )(mine)
    gathered = lax.all_to_all(copies, "x", split_axis=0, concat_axis=0, tiled=True)
    return gathered.reshape(4 * mine.shape[0], 2 * HD)


def swap(by):
    return [(source, source ^ by) for source in range(4)]


def per_device(queries, keys, values):
    packed = pack(queries, keys, values)
    mine = lax.all_to_all(packed, HEAD_GROUP, split_axis=0, concat_axis=0, tiled=True)
    mine = mine.reshape(HEADS * TOKENS, 3 * HD)
    own_q = mine[:, :HD]
    kv = spread(mine)
    query = [own_q] + [lax.ppermute(own_q, "zh", swap(by)) for by in TURNS[1:]]
    other_kv = lax.ppermute(kv, "c", [(0, 1), (1, 0)])
    me = lax.axis_index("zh").astype(jnp.int32).reshape(1)
    parts = attend(query, kv, other_kv, me)
    sent = lax.all_to_all(parts, BACK_GROUP, split_axis=0, concat_axis=0, tiled=True)
    return combine(sent)


def solution(mesh):
    fine = Mesh(mesh.devices.reshape(SIZES), AXES)
    placed = P(AXES, None)
    return jax.shard_map(
        per_device, mesh=fine, in_specs=(placed,) * 3, out_specs=placed, check_vma=False
    )
```
